128 devices in a mesh: tm: 32 (over z, y, x_lo), slab: 4 (over x_hi, core).
Axes of the slice: x: 4 (x_hi: 2, x_lo: 2; x = x_hi * 2 + x_lo), y: 4, z: 4, core: 2. Of those that a mesh axis runs over, the one named last changes fastest.
Arguments:
- kspace: bfloat16 [2, 64, 4, 96, 9984], P(None, 'tm', None, 'slab'), may hold values from -40 to 40, as said below
- sens: float32 [2, 4, 8, 104, 96], P(None, None, None, 'slab'), may hold values from -3 to 3
Outputs:
- projected: float32 [64, 2, 8, 104, 96], P('tm', None, None, 'slab')
The draws below stay inside these ranges and needn't reach their ends.
Inputs may be any that keep to these rules, and one draw needn't show every extreme that they name: `kspace`: k-space values of order one with frames of different scale.
All inputs are finite; a program needn't handle non-finite values.
Results may differ from the reference program's by a relative error of at most 0.0036.
Values may be sent and summed in bfloat16 or wider, within the bound.
A program may use at most 128 MiB of HBM per device.

```python
from functools import partial
import jax
import jax.numpy as jnp
from jax import lax

NX = 96
NY = 104
NZ = 96
COILS = 4
RANK = 32
ITERS = 4
XW = 8
FR = 2
FRAMES = 64
N_TM = 32


def draw_kspace(key, part):
    shared_key, frame_key, scale_key = jax.random.split(key, 3)
    shared = jax.random.normal(shared_key, (2, 1, COILS, NZ, NX * NY), jnp.float32)
    varying = jax.random.normal(frame_key, (2, FRAMES, COILS, NZ, NX * NY), jnp.float32)
    spread = jnp.exp(jax.random.uniform(scale_key, (1, FRAMES, 1, 1, 1), jnp.float32, -1.2, 1.2))
    return (shared + spread * varying).astype(jnp.bfloat16)


def steps_of(rng, shape, pieces, least, largest):
    factor_of = 1.0
    for dim, parts in pieces:
        draws = jax.random.uniform(jax.random.fold_in(jax.random.fold_in(rng, 6), dim), (parts,), jnp.float32, least / len(pieces), largest / len(pieces))
        factor_of = factor_of * jnp.repeat(jnp.exp(draws), shape[dim] // parts).reshape((-1,) + (1,) * (len(shape) - 1 - dim))
    return factor_of


def noise(own_key, shape, scale, bound, shards=(), kind=jnp.bfloat16):
    factor_of = steps_of(own_key, shape, shards, -0.22, 0.18) if shards else 1.0
    entries = jax.random.normal(own_key, shape, jnp.float32) * scale * factor_of
    return jnp.minimum(jnp.maximum(entries, -bound), bound).astype(kind)


def setup_inputs(seed: int = 0) -> dict:
    arg_keys = jax.random.split(jax.random.key(seed), 3)
    kspace = draw_kspace(jax.random.fold_in(arg_keys[2], 71), 0)
    sens = noise(arg_keys[1], (2, COILS, XW, NY, NZ), 0.5, 3.0, ((3, 4),), jnp.float32)
    return {"kspace": kspace, "sens": sens}


def image_column(frame, sens):
    spectrum = (frame[0].astype(jnp.float32) + 1j * frame[1].astype(jnp.float32)).reshape(COILS, NZ, NX, NY)
    planes = jnp.fft.ifft2(spectrum, axes=(2, 3), norm='ortho')
    offset = (NX - XW) // 2
    planes = planes[:, :, offset:offset + XW, :]
    kept_real, kept_other = lax.optimization_barrier((planes.real.astype(jnp.bfloat16), planes.imag.astype(jnp.bfloat16)))
    rounded = kept_real.astype(jnp.float32) + 1j * kept_other.astype(jnp.float32)
    volume = jnp.fft.ifft(rounded, axis=1, norm='ortho')
    volume = jnp.transpose(volume, (0, 2, 3, 1))
    coil_maps = sens[0] + 1j * sens[1]
    combined = jnp.sum(jnp.conj(coil_maps) * volume, axis=0)
    return jnp.concatenate([combined.real.reshape(-1), combined.imag.reshape(-1)]).astype(jnp.float32)

def matmul(left, right):
    return jnp.dot(left, right, precision=lax.Precision.HIGHEST)

def orthonormal(rows):
    factor = jnp.linalg.cholesky(matmul(rows, rows.T))
    return lax.linalg.triangular_solve(factor, rows, left_side=True, lower=True)

def truncate(pair):
    stacked = jnp.concatenate([pair[0], pair[1]], axis=0)
    current = pair[0] + pair[1]
    for sweep_index in range(ITERS):
        qrows = orthonormal(current)
        current = matmul(matmul(qrows, stacked.T), stacked)
    qrows = orthonormal(current)
    correlation = matmul(qrows, stacked.T)
    coupling = jnp.linalg.cholesky(matmul(correlation, correlation.T))
    return matmul(coupling.T, qrows)

def reference(kspace, sens):
    frames_first = jnp.moveaxis(kspace, 1, 0)
    matrix = lax.map(partial(image_column, sens=sens), frames_first)
    width = matrix.shape[1]
    nodes = matrix.reshape(N_TM, FR, width)
    count = N_TM
    columns = FR
    while count > 1:
        pairs = nodes.reshape(count // 2, 2, columns, width)
        if 2 * columns <= RANK:
            columns = 2 * columns
            nodes = pairs.reshape(count // 2, columns, width)
        else:
            columns = RANK
            nodes = lax.map(truncate, pairs)
        count = count // 2
    root_rows = orthonormal(nodes[0])
    loadings = matmul(matrix, root_rows.T)
    projected = matmul(loadings, root_rows)
    return projected.reshape(FRAMES, 2, XW, NY, NZ)
```

```python
import jax
import jax.numpy as jnp
from jax import lax
from jax.sharding import PartitionSpec as P

NX = 96
NY = 104
NZ = 96
RANK = 32
ITERS = 4
XW = 8


def inverse_table(length, count, offset):
    outputs = jnp.arange(count, dtype=jnp.int32) + offset
    inputs = jnp.arange(length, dtype=jnp.int32)
    phase = outputs[:, None] * inputs[None, :] % length
    angle = phase.astype(jnp.float32) * (2.0 * jnp.pi / length)
    norm_factor = 1.0 / jnp.sqrt(jnp.float32(length))
    return (jnp.cos(angle) * norm_factor, jnp.sin(angle) * norm_factor)


def contract(pattern, matrix_table, operand):
    return jnp.einsum(pattern, matrix_table, operand, precision=lax.Precision.HIGHEST)


def matmul(left, right):
    return jnp.dot(left, right, precision=lax.Precision.HIGHEST)


def orthonormal(rows, gram):
    factor = jnp.linalg.cholesky(matmul(matmul(rows, gram), rows.T))
    return lax.linalg.triangular_solve(factor, rows, left_side=True, lower=True)


def local(kspace, sens):
    frames_dev = kspace.shape[1]
    coil_count = kspace.shape[2]
    depth_dev = kspace.shape[3]
    spectrum = kspace.astype(jnp.float32).reshape(2, frames_dev, coil_count, depth_dev, NX, NY)
    across_cos, across_sin = inverse_table(NX, XW, (NX - XW) // 2)
    down_cos, down_sin = inverse_table(NY, NY, 0)
    depth_cos, depth_sin = inverse_table(NZ, NZ, 0)
    across_real = contract("jx,fczxy->fczjy", across_cos, spectrum[0]) - contract(
        "jx,fczxy->fczjy", across_sin, spectrum[1]
    )
    across_other = contract("jx,fczxy->fczjy", across_cos, spectrum[1]) + contract(
        "jx,fczxy->fczjy", across_sin, spectrum[0]
    )
    down_real = contract("my,fczjy->fczjm", down_cos, across_real) - contract(
        "my,fczjy->fczjm", down_sin, across_other
    )
    down_other = contract("my,fczjy->fczjm", down_cos, across_other) + contract(
        "my,fczjy->fczjm", down_sin, across_real
    )
    planes = jnp.stack([down_real, down_other]).astype(jnp.bfloat16)
    arrived = lax.all_to_all(planes, "slab", split_axis=5, concat_axis=3, tiled=True).astype(
        jnp.float32
    )
    depth_real = contract("wz,fczxy->fcxyw", depth_cos, arrived[0]) - contract(
        "wz,fczxy->fcxyw", depth_sin, arrived[1]
    )
    depth_other = contract("wz,fczxy->fcxyw", depth_cos, arrived[1]) + contract(
        "wz,fczxy->fcxyw", depth_sin, arrived[0]
    )
    sens_real = sens[0][None]
    sens_other = sens[1][None]
    combined_real = jnp.sum(sens_real * depth_real + sens_other * depth_other, axis=1)
    combined_other = jnp.sum(sens_real * depth_other - sens_other * depth_real, axis=1)
    matrix = jnp.stack([combined_real, combined_other], axis=1).reshape(frames_dev, -1)
    rows = lax.all_to_all(matrix, "tm", split_axis=1, concat_axis=0, tiled=True)
    gram = lax.psum(matmul(rows, rows.T), ("tm", "slab"))
    eye = jnp.eye(RANK, dtype=jnp.float32)
    current = jnp.concatenate([eye, eye], axis=1)
    for sweep_index in range(ITERS):
        current = matmul(orthonormal(current, gram), gram)
    coeff = orthonormal(current, gram)
    mixing = matmul(matmul(coeff, gram).T, coeff)
    projected = matmul(mixing, rows)
    projected = lax.all_to_all(projected, "tm", split_axis=0, concat_axis=1, tiled=True)
    return projected.reshape(frames_dev, 2, XW, -1, NZ)


def solution(mesh):
    in_specs = (P(None, "tm", None, "slab", None), P(None, None, None, "slab", None))
    out_specs = P("tm", None, None, "slab", None)
    return jax.shard_map(local, mesh=mesh, in_specs=in_specs, out_specs=out_specs, check_vma=False)
```

```python
import jax
import jax.numpy as jnp
from jax import lax
from jax.experimental import pallas as pl
from jax.experimental.pallas import tpu as pltpu
from jax.sharding import PartitionSpec as P

NX = 96
NY = 104
NZ = 96
RANK = 32
ITERS = 4
XW = 8
FRAMES = 64


def inverse_table(length, count, offset):
    outputs = jnp.arange(count, dtype=jnp.int32) + offset
    inputs = jnp.arange(length, dtype=jnp.int32)
    phase = outputs[:, None] * inputs[None, :] % length
    angle = phase.astype(jnp.float32) * (2.0 * jnp.pi / length)
    norm_factor = 1.0 / jnp.sqrt(jnp.float32(length))
    return (jnp.cos(angle) * norm_factor, jnp.sin(angle) * norm_factor)


def contract(pattern, matrix_table, operand):
    return jnp.einsum(pattern, matrix_table, operand, precision=lax.Precision.HIGHEST)


def matmul(left, right):
    return jnp.dot(left, right, precision=lax.Precision.HIGHEST)


def wait_bytes(ref, sem):
    pltpu.make_async_copy(ref, ref, sem).wait()


def eliminate(table, extra):
    row = lax.broadcasted_iota(jnp.int32, (RANK, 1), 0)
    for k in range(RANK):
        pivot_row = table[k : k + 1, :]
        factor = table[:, k : k + 1] * (1.0 / pivot_row[:, k : k + 1])
        factor = jnp.where(row > k, factor, 0.0)
        extra = extra - factor * extra[k : k + 1, :]
        table = table - factor * pivot_row
    lane = lax.broadcasted_iota(jnp.int32, (RANK, 128), 1)
    rows = lax.broadcasted_iota(jnp.int32, (RANK, 128), 0)
    diagonal = jnp.sum(jnp.where(lane == rows, table, 0.0), axis=1, keepdims=True)
    scale = lax.rsqrt(diagonal)
    return table * scale, extra * scale


def dot_t(left, right):
    return lax.dot_general(
        left,
        right,
        (((1,), (1,)), ((), ())),
        precision=lax.Precision.HIGHEST,
        preferred_element_type=jnp.float32,
    )


def root_coefficients(gram):
    def sweep(_, state):
        weights, _ = state
        image = matmul(weights, gram)
        inner = dot_t(image, weights)
        pad = jnp.zeros((RANK, 32), jnp.float32)
        pad_wide = jnp.zeros((RANK, 64), jnp.float32)
        table, extra = eliminate(
            jnp.concatenate([inner, image, pad], axis=1),
            jnp.concatenate([weights, pad_wide], axis=1),
        )
        return table[:, RANK : RANK + FRAMES], extra[:, :FRAMES]

    lane = lax.broadcasted_iota(jnp.int32, (RANK, FRAMES), 1)
    row = lax.broadcasted_iota(jnp.int32, (RANK, FRAMES), 0)
    start = jnp.where(lane % RANK == row, 1.0, 0.0).astype(jnp.float32)
    return lax.fori_loop(0, ITERS + 1, sweep, (start, start))


def merge_kernel(flip, m_ref, out_ref, recv, whole, outf, outb, gx, gy, gz, sems):
    me = lax.axis_index("tm")
    slab = lax.axis_index("slab")
    x_lo = me % 2
    y_pos = (me // 2) % 4
    z_pos = me // 8
    owner = me + 1 - 2 * x_lo if flip else me
    x_pos = slab * 2 + x_lo

    def tm_peer(k):
        return (lax.rem(me + k, 32), slab)

    def x_peer(k):
        other = lax.rem(x_pos + k, 8)
        return (me - x_lo + other % 2, other // 2)

    def y_peer(k):
        return (z_pos * 8 + lax.rem(y_pos + k, 4) * 2 + x_lo, slab)

    def z_peer(k):
        return (lax.rem(z_pos + k, 4) * 8 + y_pos * 2 + x_lo, slab)

    barrier = pltpu.get_barrier_semaphore()

    def greet(peer):
        pl.semaphore_signal(barrier, inc=1, device_id=peer, device_id_type=pl.DeviceIdType.MESH)

    lax.fori_loop(1, 32, lambda k, c: (greet(tm_peer(k)), c)[1], 0)
    lax.fori_loop(1, 8, lambda k, c: (greet(x_peer(k)), c)[1], 0)
    pl.semaphore_wait(barrier, 38)

    def send(src, dst, send_sem, recv_sem, peer):
        pltpu.make_async_remote_copy(
            src_ref=src,
            dst_ref=dst,
            send_sem=send_sem,
            recv_sem=recv_sem,
            device_id=peer,
            device_id_type=pl.DeviceIdType.MESH,
        ).start()

    def scatter(k, c):
        peer = tm_peer(k)
        first = pl.multiple_of(peer[0] * 16, 16)
        send(
            m_ref.at[:, pl.ds(first, 16), :],
            recv.at[pl.ds(2 * owner, 2)],
            sems.at[0],
            sems.at[1],
            peer,
        )
        return c

    lax.fori_loop(1, 32, scatter, 0)
    mine = pl.multiple_of(me * 16, 16)
    recv[pl.ds(2 * owner, 2)] = m_ref[:, pl.ds(mine, 16), :]
    wait_bytes(m_ref.at[:, pl.ds(0, 31 * 16), :], sems.at[0])
    wait_bytes(recv.at[pl.ds(0, 62)], sems.at[1])
    flat = recv.reshape(FRAMES * 16, 128)
    for i in range(16):
        whole[:, i * 128 : (i + 1) * 128] = flat[pl.ds(i, FRAMES, stride=16), :]
    gram = dot_t(whole[...], whole[...])
    packed = jnp.concatenate([gram[:32], gram[32:]], axis=1)

    def all_sum(value, buf, pos, count, peer_of, sem_at):
        buf[pl.ds(pos, 1)] = value[None]
        for k in range(1, count):
            send(buf.at[pl.ds(pos, 1)], buf.at[pl.ds(pos, 1)], sems.at[sem_at], sems.at[sem_at + 1], peer_of(k))
        wait_bytes(buf.at[pl.ds(0, count - 1)], sems.at[sem_at])
        wait_bytes(buf.at[pl.ds(0, count - 1)], sems.at[sem_at + 1])
        total = buf[0]
        for k in range(1, count):
            total = total + buf[k]
        return total

    packed = all_sum(packed, gx, x_pos, 8, x_peer, 2)
    packed = all_sum(packed, gy, y_pos, 4, y_peer, 4)
    packed = all_sum(packed, gz, z_pos, 4, z_peer, 6)
    gram = jnp.concatenate([packed[:, :64], packed[:, 64:]], axis=0)
    image, coeff = root_coefficients(gram)
    mixing = lax.dot_general(
        image,
        coeff,
        (((0,), (0,)), ((), ())),
        precision=lax.Precision.HIGHEST,
        preferred_element_type=jnp.float32,
    )
    for i in range(16):
        outf[pl.ds(i, FRAMES, stride=16), :] = matmul(mixing, whole[:, i * 128 : (i + 1) * 128])
    outb[...] = outf[...].reshape(FRAMES, 16, 128).astype(jnp.bfloat16)

    def give(k, c):
        peer = tm_peer(k)
        send(
            outb.at[pl.ds(2 * peer[0], 2)],
            out_ref.at[:, pl.ds(mine, 16), :],
            sems.at[8],
            sems.at[9],
            peer,
        )
        return c

    lax.fori_loop(1, 32, give, 0)
    out_ref[:, pl.ds(mine, 16), :] = outb[pl.ds(2 * me, 2)]
    wait_bytes(outb.at[pl.ds(0, 62)], sems.at[8])
    wait_bytes(out_ref.at[:, pl.ds(0, 31 * 16), :], sems.at[9])


def merge(m, flip):
    return pl.pallas_call(
        lambda *refs: merge_kernel(flip, *refs),
        out_shape=jax.ShapeDtypeStruct((2, 512, 128), jnp.bfloat16),
        in_specs=[pl.BlockSpec(memory_space=pltpu.VMEM)],
        out_specs=pl.BlockSpec(memory_space=pltpu.VMEM),
        scratch_shapes=[
            pltpu.VMEM((FRAMES, 16, 128), jnp.float32),
            pltpu.VMEM((FRAMES, 2048), jnp.float32),
            pltpu.VMEM((FRAMES * 16, 128), jnp.float32),
            pltpu.VMEM((FRAMES, 16, 128), jnp.bfloat16),
            pltpu.VMEM((8, 32, 128), jnp.float32),
            pltpu.VMEM((4, 32, 128), jnp.float32),
            pltpu.VMEM((4, 32, 128), jnp.float32),
            pltpu.SemaphoreType.DMA((10,)),
        ],
        compiler_params=pltpu.CompilerParams(
            collective_id=0, has_side_effects=True, vmem_limit_bytes=40 * 1024 * 1024
        ),
        name="merge",
    )(m)


def local(kspace, sens):
    frames_dev = kspace.shape[1]
    coil_count = kspace.shape[2]
    depth_dev = kspace.shape[3]
    spectrum = kspace.astype(jnp.float32).reshape(2, frames_dev, coil_count, depth_dev, NX, NY)
    across_cos, across_sin = inverse_table(NX, XW, (NX - XW) // 2)
    down_cos, down_sin = inverse_table(NY, NY, 0)
    depth_cos, depth_sin = inverse_table(NZ, NZ, 0)
    across_real = contract("jx,fczxy->fczjy", across_cos, spectrum[0]) - contract(
        "jx,fczxy->fczjy", across_sin, spectrum[1]
    )
    across_other = contract("jx,fczxy->fczjy", across_cos, spectrum[1]) + contract(
        "jx,fczxy->fczjy", across_sin, spectrum[0]
    )
    down_real = contract("my,fczjy->fczjm", down_cos, across_real) - contract(
        "my,fczjy->fczjm", down_sin, across_other
    )
    down_other = contract("my,fczjy->fczjm", down_cos, across_other) + contract(
        "my,fczjy->fczjm", down_sin, across_real
    )
    planes = jnp.stack([down_real, down_other]).astype(jnp.bfloat16)
    arrived = lax.all_to_all(planes, "slab", split_axis=5, concat_axis=3, tiled=True).astype(
        jnp.float32
    )
    depth_real = contract("wz,fczxy->fcxyw", depth_cos, arrived[0]) - contract(
        "wz,fczxy->fcxyw", depth_sin, arrived[1]
    )
    depth_other = contract("wz,fczxy->fcxyw", depth_cos, arrived[1]) + contract(
        "wz,fczxy->fcxyw", depth_sin, arrived[0]
    )
    sens_real = sens[0][None]
    sens_other = sens[1][None]
    combined_real = jnp.sum(sens_real * depth_real + sens_other * depth_other, axis=1)
    combined_other = jnp.sum(sens_real * depth_other - sens_other * depth_real, axis=1)
    matrix = jnp.stack([combined_real, combined_other], axis=1).transpose(0, 3, 1, 2, 4)
    matrix = jnp.pad(matrix, ((0, 0), (0, 6), (0, 0), (0, 0), (0, 32))).reshape(2, 512, 128)
    projected = merge(matrix, False).reshape(2, 32, 2, XW, 128)
    projected = projected[:, :26, :, :, :NZ].astype(jnp.float32)
    return projected.transpose(0, 2, 3, 1, 4)


def solution(mesh):
    in_specs = (P(None, "tm", None, "slab", None), P(None, None, None, "slab", None))
    out_specs = P("tm", None, None, "slab", None)
    return jax.shard_map(local, mesh=mesh, in_specs=in_specs, out_specs=out_specs, check_vma=False)
```

```python
import jax
import jax.numpy as jnp
import ml_dtypes
import numpy as np
from jax import lax
from jax.experimental import pallas as pl
from jax.experimental.pallas import tpu as pltpu
from jax.sharding import PartitionSpec as P

NX = 96
NY = 104
NZ = 96
RANK = 32
ITERS = 4
XW = 8
FRAMES = 64


def matmul(left, right):
    return jnp.dot(left, right, precision=lax.Precision.HIGHEST)


def wait_bytes(ref, sem):
    pltpu.make_async_copy(ref, ref, sem).wait()


def eliminate(table, extra):
    row = lax.broadcasted_iota(jnp.int32, (RANK, 1), 0)
    for k in range(RANK):
        pivot_row = table[k : k + 1, :]
        factor = table[:, k : k + 1] * (1.0 / pivot_row[:, k : k + 1])
        factor = jnp.where(row > k, factor, 0.0)
        extra = extra - factor * extra[k : k + 1, :]
        table = table - factor * pivot_row
    lane = lax.broadcasted_iota(jnp.int32, (RANK, 128), 1)
    rows = lax.broadcasted_iota(jnp.int32, (RANK, 128), 0)
    diagonal = jnp.sum(jnp.where(lane == rows, table, 0.0), axis=1, keepdims=True)
    scale = lax.rsqrt(diagonal)
    return table * scale, extra * scale


def dot_t(left, right):
    return lax.dot_general(
        left,
        right,
        (((1,), (1,)), ((), ())),
        precision=lax.Precision.HIGHEST,
        preferred_element_type=jnp.float32,
    )


def root_coefficients(gram):
    def sweep(_, state):
        weights, _ = state
        image = matmul(weights, gram)
        inner = dot_t(image, weights)
        pad = jnp.zeros((RANK, 32), jnp.float32)
        pad_wide = jnp.zeros((RANK, 64), jnp.float32)
        table, extra = eliminate(
            jnp.concatenate([inner, image, pad], axis=1),
            jnp.concatenate([weights, pad_wide], axis=1),
        )
        return table[:, RANK : RANK + FRAMES], extra[:, :FRAMES]

    lane = lax.broadcasted_iota(jnp.int32, (RANK, FRAMES), 1)
    row = lax.broadcasted_iota(jnp.int32, (RANK, FRAMES), 0)
    start = jnp.where(lane % RANK == row, 1.0, 0.0).astype(jnp.float32)
    return lax.fori_loop(0, ITERS + 1, sweep, (start, start))


def merge_kernel(flip, m_ref, out_ref, recv, whole, outf, outb, gx, gy, gz, sems):
    me = lax.axis_index("tm")
    slab = lax.axis_index("slab")
    x_lo = me % 2
    y_pos = (me // 2) % 4
    z_pos = me // 8
    owner = me + 1 - 2 * x_lo if flip else me
    x_pos = slab * 2 + x_lo

    def tm_peer(k):
        return (lax.rem(me + k, 32), slab)

    def x_peer(k):
        other = lax.rem(x_pos + k, 8)
        return (me - x_lo + other % 2, other // 2)

    def y_peer(k):
        return (z_pos * 8 + lax.rem(y_pos + k, 4) * 2 + x_lo, slab)

    def z_peer(k):
        return (lax.rem(z_pos + k, 4) * 8 + y_pos * 2 + x_lo, slab)

    barrier = pltpu.get_barrier_semaphore()

    def greet(peer):
        pl.semaphore_signal(barrier, inc=1, device_id=peer, device_id_type=pl.DeviceIdType.MESH)

    lax.fori_loop(1, 32, lambda k, c: (greet(tm_peer(k)), c)[1], 0)
    lax.fori_loop(1, 8, lambda k, c: (greet(x_peer(k)), c)[1], 0)
    pl.semaphore_wait(barrier, 38)

    def send(src, dst, send_sem, recv_sem, peer):
        pltpu.make_async_remote_copy(
            src_ref=src,
            dst_ref=dst,
            send_sem=send_sem,
            recv_sem=recv_sem,
            device_id=peer,
            device_id_type=pl.DeviceIdType.MESH,
        ).start()

    def scatter(k, c):
        peer = tm_peer(k)
        first = pl.multiple_of(peer[0] * 16, 16)
        send(
            m_ref.at[:, pl.ds(first, 16), :],
            recv.at[pl.ds(2 * owner, 2)],
            sems.at[0],
            sems.at[1],
            peer,
        )
        return c

    lax.fori_loop(1, 32, scatter, 0)
    mine = pl.multiple_of(me * 16, 16)
    recv[pl.ds(2 * owner, 2)] = m_ref[:, pl.ds(mine, 16), :]
    wait_bytes(m_ref.at[:, pl.ds(0, 31 * 16), :], sems.at[0])
    wait_bytes(recv.at[pl.ds(0, 62)], sems.at[1])
    flat = recv.reshape(FRAMES * 16, 128)
    for i in range(16):
        whole[:, i * 128 : (i + 1) * 128] = flat[pl.ds(i, FRAMES, stride=16), :]
    gram = dot_t(whole[...], whole[...])
    packed = jnp.concatenate([gram[:32], gram[32:]], axis=1)

    def all_sum(value, buf, pos, count, peer_of, sem_at):
        buf[pl.ds(pos, 1)] = value[None]
        for k in range(1, count):
            send(buf.at[pl.ds(pos, 1)], buf.at[pl.ds(pos, 1)], sems.at[sem_at], sems.at[sem_at + 1], peer_of(k))
        wait_bytes(buf.at[pl.ds(0, count - 1)], sems.at[sem_at])
        wait_bytes(buf.at[pl.ds(0, count - 1)], sems.at[sem_at + 1])
        total = buf[0]
        for k in range(1, count):
            total = total + buf[k]
        return total

    packed = all_sum(packed, gx, x_pos, 8, x_peer, 2)
    packed = all_sum(packed, gy, y_pos, 4, y_peer, 4)
    packed = all_sum(packed, gz, z_pos, 4, z_peer, 6)
    gram = jnp.concatenate([packed[:, :64], packed[:, 64:]], axis=0)
    image, coeff = root_coefficients(gram)
    mixing = lax.dot_general(
        image,
        coeff,
        (((0,), (0,)), ((), ())),
        precision=lax.Precision.HIGHEST,
        preferred_element_type=jnp.float32,
    )
    for i in range(16):
        outf[pl.ds(i, FRAMES, stride=16), :] = matmul(mixing, whole[:, i * 128 : (i + 1) * 128])
    outb[...] = outf[...].reshape(FRAMES, 16, 128).astype(jnp.bfloat16)

    def give(k, c):
        peer = tm_peer(k)
        send(
            outb.at[pl.ds(2 * peer[0], 2)],
            out_ref.at[:, pl.ds(mine, 16), :],
            sems.at[8],
            sems.at[9],
            peer,
        )
        return c

    lax.fori_loop(1, 32, give, 0)
    out_ref[:, pl.ds(mine, 16), :] = outb[pl.ds(2 * me, 2)]
    wait_bytes(outb.at[pl.ds(0, 62)], sems.at[8])
    wait_bytes(out_ref.at[:, pl.ds(0, 31 * 16), :], sems.at[9])


def merge(m, flip):
    return pl.pallas_call(
        lambda *refs: merge_kernel(flip, *refs),
        out_shape=jax.ShapeDtypeStruct((2, 512, 128), jnp.bfloat16),
        in_specs=[pl.BlockSpec(memory_space=pltpu.VMEM)],
        out_specs=pl.BlockSpec(memory_space=pltpu.VMEM),
        scratch_shapes=[
            pltpu.VMEM((FRAMES, 16, 128), jnp.float32),
            pltpu.VMEM((FRAMES, 2048), jnp.float32),
            pltpu.VMEM((FRAMES * 16, 128), jnp.float32),
            pltpu.VMEM((FRAMES, 16, 128), jnp.bfloat16),
            pltpu.VMEM((8, 32, 128), jnp.float32),
            pltpu.VMEM((4, 32, 128), jnp.float32),
            pltpu.VMEM((4, 32, 128), jnp.float32),
            pltpu.SemaphoreType.DMA((10,)),
        ],
        compiler_params=pltpu.CompilerParams(
            collective_id=0, has_side_effects=True, vmem_limit_bytes=40 * 1024 * 1024
        ),
        name="merge",
    )(m)


def split_bf16(table):
    high = table.astype(ml_dtypes.bfloat16)
    low = (table - high.astype(np.float64)).astype(ml_dtypes.bfloat16)
    return high, low


def across_table():
    x = np.arange(XW) + (NX - XW) // 2
    angle = 2.0 * np.pi * (x[:, None] * np.arange(NX)[None, :] % NX) / NX
    cos, sin = np.cos(angle) / np.sqrt(NX), np.sin(angle) / np.sqrt(NX)
    table = np.zeros((XW, 2, 8, NX, 2, 8))
    for r in range(8):
        table[:, 0, r, :, 0, r] = cos
        table[:, 0, r, :, 1, r] = -sin
        table[:, 1, r, :, 0, r] = sin
        table[:, 1, r, :, 1, r] = cos
    return np.concatenate(split_bf16(table.reshape(XW * 16, NX * 16)), axis=0)


def down_table():
    angle = 2.0 * np.pi * (np.arange(NY)[:, None] * np.arange(NY)[None, :] % NY) / NY
    table = np.zeros((4, 32, 2, 128))
    table[:, :26, 0, :NY] = np.cos(angle).reshape(4, 26, NY) / np.sqrt(NY)
    table[:, :26, 1, :NY] = np.sin(angle).reshape(4, 26, NY) / np.sqrt(NY)
    return np.concatenate(split_bf16(table.reshape(128, 256)), axis=0)


def depth_table():
    angle = 2.0 * np.pi * (np.arange(NZ)[:, None] * np.arange(NZ)[None, :] % NZ) / NZ
    cos = (np.cos(angle) / np.sqrt(NZ)).reshape(4, 24, NZ)
    sin = (np.sin(angle) / np.sqrt(NZ)).reshape(4, 24, NZ)
    table = np.zeros((4, 2, 4, 24, 4, 2, 128))
    for c in range(4):
        table[:, 0, c, :, c, 0, :NZ] = cos
        table[:, 1, c, :, c, 0, :NZ] = -sin
        table[:, 0, c, :, c, 1, :NZ] = sin
        table[:, 1, c, :, c, 1, :NZ] = cos
    full = np.zeros((4, 320, 1024))
    full[:, 64:256] = table.reshape(4, 192, 1024)
    return np.stack(split_bf16(full))


def front_kernel(
    k_ref, sens_ref, across_ref, down_ref, depth_ref, m_ref,
    data, spec_hi, spec_lo, sent, got, depth, acc, data_sems, depth_sem, sems,
):
    me = lax.axis_index("tm")
    slab = lax.axis_index("slab")
    mirror = me + 1 - 2 * (me % 2)

    def fetch(g):
        rows = pl.ds(pl.multiple_of(g * 16, 16), 16)
        return pltpu.make_async_copy(k_ref.at[:, rows, :], data.at[:, rows, :], data_sems.at[g])

    def begin(g, c):
        fetch(g).start()
        return c

    lax.fori_loop(0, 12, begin, 0)
    depth_copy = pltpu.make_async_copy(depth_ref, depth, depth_sem)
    depth_copy.start()
    barrier = pltpu.get_barrier_semaphore()
    for s in range(4):
        pl.semaphore_signal(
            barrier, inc=1, device_id=(mirror, s), device_id_type=pl.DeviceIdType.MESH
        )
    m_ref[...] = jnp.zeros_like(m_ref)

    def across(g, c):
        fetch(g).wait()
        rows = pl.ds(pl.multiple_of(g * 16, 16), 16)
        place = pl.multiple_of(lax.rem(g, 6) * 16, 16)
        total = jnp.zeros((256, 256), jnp.float32)
        for t in range(6):
            lo, hi = t * 1664, (t + 1) * 1664
            real = data[0, rows, lo:hi].astype(jnp.float32)
            other = data[1, rows, lo:hi].astype(jnp.float32)
            parts = []
            for h in range(2):
                both = jnp.concatenate(
                    [real[h * 8 : h * 8 + 8], other[h * 8 : h * 8 + 8]], axis=0
                ).astype(jnp.bfloat16)
                both = jnp.concatenate([both, jnp.zeros((16, 128), jnp.bfloat16)], axis=1)
                parts.append(
                    jnp.concatenate([both[:, a * 104 : a * 104 + 128] for a in range(16)], axis=0)
                )
            total = total + jnp.dot(
                across_ref[:, t * 256 : (t + 1) * 256],
                jnp.concatenate(parts, axis=1),
                preferred_element_type=jnp.float32,
            )
        image = total[:128] + total[128:]
        for j in range(XW):
            real = jnp.concatenate([image[j * 16 : j * 16 + 8, h * 128 : h * 128 + 128] for h in range(2)], axis=0)
            other = jnp.concatenate([image[j * 16 + 8 : j * 16 + 16, h * 128 : h * 128 + 128] for h in range(2)], axis=0)
            for part, pair in ((0, (real, -other)), (1, (other, real))):
                value = jnp.concatenate(pair, axis=1)
                high = value.astype(jnp.bfloat16)
                low = (value - high.astype(jnp.float32)).astype(jnp.bfloat16)
                at = pl.ds(place + ((j % 2) * 192 + part * 96), 16)
                spec_hi[j // 2, at, :] = high
                spec_lo[j // 2, at, :] = low
        return c

    def down(f):
        for jp in range(4):
            dims = (((1,), (1,)), ((), ()))
            first = lax.dot_general(down_ref[...], spec_hi[jp], dims, preferred_element_type=jnp.float32)
            second = lax.dot_general(down_ref[:128, :], spec_lo[jp], dims, preferred_element_type=jnp.float32)
            planes = (first[:128] + first[128:] + second).astype(jnp.bfloat16)
            for s in range(4):
                sent[f, s, jp * 32 : jp * 32 + 32, :] = planes[s * 32 : s * 32 + 32]

    def copy(f, s):
        return pltpu.make_async_remote_copy(
            src_ref=sent.at[f, s],
            dst_ref=got.at[f, slab],
            send_sem=sems.at[f],
            recv_sem=sems.at[2 + f],
            device_id=(mirror, s),
            device_id_type=pl.DeviceIdType.MESH,
        )

    for f in range(2):
        lax.fori_loop(6 * f, 6 * f + 6, across, 0)
        down(f)
        if f == 0:
            pl.semaphore_wait(barrier, 4)
        for s in range(4):
            copy(f, s).start()
    depth_copy.wait()
    for f in range(2):
        wait_bytes(got.at[f], sems.at[2 + f])
        for j2 in range(2):
            total = None
            for q in range(4):
                window = got[f, q, :, j2 * 128 : j2 * 128 + 256]
                for h in range(2):
                    term = jnp.dot(
                        window,
                        depth[h, q, 64 - 64 * j2 : 320 - 64 * j2, :],
                        preferred_element_type=jnp.float32,
                    )
                    total = term if total is None else total + term
            acc[...] = total

            def combine(jp, c, j2=j2, f=f):
                j = jp * 2 + j2
                real = other = None
                for coil in range(4):
                    rows = pl.ds(pl.multiple_of(jp * 32, 32), 32)
                    wave_real = acc[rows, coil * 256 : coil * 256 + 96][:26]
                    wave_other = acc[rows, coil * 256 + 128 : coil * 256 + 224][:26]
                    sens_real = sens_ref[0, coil, pl.ds(j, 26, stride=8), :]
                    sens_other = sens_ref[1, coil, pl.ds(j, 26, stride=8), :]
                    term_real = sens_real * wave_real + sens_other * wave_other
                    term_other = sens_real * wave_other - sens_other * wave_real
                    real = term_real if real is None else real + term_real
                    other = term_other if other is None else other + term_other
                pad = ((0, 0), (0, 32))
                m_ref[f, pl.ds(j, 26, stride=16), :] = jnp.pad(real, pad)
                m_ref[f, pl.ds(j + 8, 26, stride=16), :] = jnp.pad(other, pad)
                return c

            lax.fori_loop(0, 4, combine, 0)
    for f in range(2):
        wait_bytes(sent.at[f], sems.at[f])


def front(kspace, sens):
    any_spec = pl.BlockSpec(memory_space=pl.ANY)
    vmem_spec = pl.BlockSpec(memory_space=pltpu.VMEM)
    return pl.pallas_call(
        front_kernel,
        out_shape=jax.ShapeDtypeStruct((2, 512, 128), jnp.float32),
        in_specs=[any_spec, vmem_spec, vmem_spec, vmem_spec, any_spec],
        out_specs=vmem_spec,
        scratch_shapes=[
            pltpu.VMEM((2, 192, 9984), jnp.bfloat16),
            pltpu.VMEM((4, 384, 256), jnp.bfloat16),
            pltpu.VMEM((4, 384, 256), jnp.bfloat16),
            pltpu.VMEM((2, 4, 128, 384), jnp.bfloat16),
            pltpu.VMEM((2, 4, 128, 384), jnp.bfloat16),
            pltpu.VMEM((2, 4, 320, 1024), jnp.bfloat16),
            pltpu.VMEM((128, 1024), jnp.float32),
            pltpu.SemaphoreType.DMA((12,)),
            pltpu.SemaphoreType.DMA,
            pltpu.SemaphoreType.DMA((4,)),
        ],
        compiler_params=pltpu.CompilerParams(
            collective_id=1, has_side_effects=True, vmem_limit_bytes=48 * 1024 * 1024
        ),
        name="front",
    )(
        kspace.reshape(2, 192, NX * NY),
        sens.transpose(0, 1, 3, 2, 4).reshape(2, 4, 208, NZ),
        across_table(),
        down_table(),
        depth_table(),
    )


def local(kspace, sens):
    projected = merge(front(kspace, sens), True).reshape(2, 32, 2, XW, 128)
    projected = projected[:, :26, :, :, :NZ].astype(jnp.float32)
    return projected.transpose(0, 2, 3, 1, 4)


def solution(mesh):
    in_specs = (P(None, "tm", None, "slab", None), P(None, None, None, "slab", None))
    out_specs = P("tm", None, None, "slab", None)
    return jax.shard_map(local, mesh=mesh, in_specs=in_specs, out_specs=out_specs, check_vma=False)
```

```python
import jax
import jax.numpy as jnp
import ml_dtypes
import numpy as np
from jax import lax
from jax.experimental import pallas as pl
from jax.experimental.pallas import tpu as pltpu
from jax.sharding import PartitionSpec as P

NX = 96
NY = 104
NZ = 96
RANK = 32
ITERS = 4
XW = 8
FRAMES = 64
ROWS = NY // 4
PANEL = 16


def matmul(left, right):
    return jnp.dot(
        left, right, precision=lax.Precision.HIGHEST, preferred_element_type=jnp.float32
    )


def dot_t(left, right):
    return lax.dot_general(
        left,
        right,
        (((1,), (1,)), ((), ())),
        precision=lax.Precision.HIGHEST,
        preferred_element_type=jnp.float32,
    )


def wait_bytes(ref, sem):
    pltpu.make_async_copy(ref, ref, sem).wait()


def eliminate(tables):
    tables = list(tables)
    row = lax.broadcasted_iota(jnp.int32, (RANK, 128), 0)
    lane = lax.broadcasted_iota(jnp.int32, (RANK, 128), 1)
    for k in range(0, RANK, PANEL):
        columns = [
            jnp.broadcast_to(tables[0][:, k + m : k + m + 1], (RANK, 128)) for m in range(PANEL)
        ]
        rows = [[table[k + m : k + m + 1, :] for m in range(PANEL)] for table in tables]
        for m in range(PANEL):
            inverse = 1.0 / columns[m][k + m : k + m + 1, :]
            factor = jnp.where(row > k + m, columns[m] * inverse, 0.0)
            for n in range(m + 1, PANEL):
                columns[n] = columns[n] - factor * columns[n][k + m : k + m + 1, :]
                for held in rows:
                    held[n] = held[n] - factor[k + n : k + n + 1, :] * held[m]
            for i, held in enumerate(rows):
                tables[i] = tables[i] - factor * held[m]
    diagonal = jnp.sum(jnp.where(lane == row, tables[0], 0.0), axis=1, keepdims=True)
    scale = lax.rsqrt(diagonal)
    return [table * scale for table in tables]


def root_coefficients(gram):
    pad = jnp.zeros((RANK, 32), jnp.float32)
    image = gram[:RANK] + gram[RANK:]
    inner = image[:, :RANK] + image[:, RANK:]
    for sweep in range(ITERS):
        (table,) = eliminate([jnp.concatenate([inner, image, pad], axis=1)])
        weights = table[:, RANK : RANK + FRAMES]
        image = matmul(weights, gram)
        inner = dot_t(image, weights)
    table, extra = eliminate(
        [
            jnp.concatenate([inner, image, pad], axis=1),
            jnp.concatenate([weights, pad, pad], axis=1),
        ]
    )
    return table[:, RANK : RANK + FRAMES], extra[:, :FRAMES]


def split_bf16(table):
    high = table.astype(ml_dtypes.bfloat16)
    low = (table - high.astype(np.float64)).astype(ml_dtypes.bfloat16)
    return high, low


def across_table():
    x = np.arange(XW) + (NX - XW) // 2
    angle = 2.0 * np.pi * (x[:, None] * np.arange(NX)[None, :] % NX) / NX
    cos, sin = np.cos(angle) / np.sqrt(NX), np.sin(angle) / np.sqrt(NX)
    table = np.zeros((XW, 2, 8, NX, 2, 8))
    for r in range(8):
        table[:, 0, r, :, 0, r] = cos
        table[:, 0, r, :, 1, r] = -sin
        table[:, 1, r, :, 0, r] = sin
        table[:, 1, r, :, 1, r] = cos
    return np.concatenate(split_bf16(table.reshape(XW * 16, NX * 16)), axis=0)


def down_table():
    angle = 2.0 * np.pi * (np.arange(NY)[:, None] * np.arange(NY)[None, :] % NY) / NY
    table = np.zeros((4, 32, 2, 128))
    table[:, :26, 0, :NY] = np.cos(angle).reshape(4, 26, NY) / np.sqrt(NY)
    table[:, :26, 1, :NY] = np.sin(angle).reshape(4, 26, NY) / np.sqrt(NY)
    return np.concatenate(split_bf16(table.reshape(128, 256)), axis=0)


def depth_table():
    angle = 2.0 * np.pi * (np.arange(NZ)[:, None] * np.arange(NZ)[None, :] % NZ) / NZ
    cos = (np.cos(angle) / np.sqrt(NZ)).reshape(4, 24, NZ)
    sin = (np.sin(angle) / np.sqrt(NZ)).reshape(4, 24, NZ)
    table = np.zeros((4, 2, 4, 24, 4, 2, 128))
    for c in range(4):
        table[:, 0, c, :, c, 0, :NZ] = cos
        table[:, 1, c, :, c, 0, :NZ] = -sin
        table[:, 0, c, :, c, 1, :NZ] = sin
        table[:, 1, c, :, c, 1, :NZ] = cos
    full = np.zeros((4, 320, 1024))
    full[:, 64:256] = table.reshape(4, 192, 1024)
    return np.stack(split_bf16(full))


def kernel(
    k_ref, sens_ref, across_ref, down_ref, depth_ref, out_ref,
    data, spec_hi, spec_lo, sent, got, acc, sens, across_tab, down_tab, depth,
    frames, recv, whole, outf, outb, gyz, gx, data_sems, table_sems, sems,
):
    me = lax.axis_index("tm")
    slab = lax.axis_index("slab")
    x_lo = me % 2
    mirror = me + 1 - 2 * x_lo
    x_pos = slab * 2 + x_lo
    yz_pos = me // 2

    def tm_peer(k):
        return (lax.rem(me + k, 32), slab)

    def x_peer(k):
        other = lax.rem(x_pos + k, 8)
        return (me - x_lo + other % 2, other // 2)

    def yz_peer(k):
        return (lax.rem(yz_pos + k, 16) * 2 + x_lo, slab)

    def fetch(g):
        rows = pl.ds(pl.multiple_of(g * 16, 16), 16)
        return pltpu.make_async_copy(k_ref.at[:, rows, :], data.at[:, rows, :], data_sems.at[g])

    def begin(g, c):
        fetch(g).start()
        return c

    across_copy = pltpu.make_async_copy(across_ref, across_tab, table_sems.at[0])
    down_copy = pltpu.make_async_copy(down_ref, down_tab, table_sems.at[1])
    depth_copy = pltpu.make_async_copy(depth_ref, depth, table_sems.at[2])
    sens_copy = pltpu.make_async_copy(sens_ref, sens, table_sems.at[3])
    fetch(0).start()
    across_copy.start()
    lax.fori_loop(1, 6, begin, 0)
    down_copy.start()
    lax.fori_loop(6, 12, begin, 0)
    depth_copy.start()
    sens_copy.start()

    barrier = pltpu.get_barrier_semaphore()

    def greet(peer):
        pl.semaphore_signal(barrier, inc=1, device_id=peer, device_id_type=pl.DeviceIdType.MESH)

    lax.fori_loop(1, 32, lambda k, c: (greet(tm_peer(k)), c)[1], 0)
    lax.fori_loop(1, 8, lambda k, c: (greet(x_peer(k)), c)[1], 0)
    frames[...] = jnp.zeros_like(frames)

    def send(src, dst, sem_at, peer):
        pltpu.make_async_remote_copy(
            src_ref=src,
            dst_ref=dst,
            send_sem=sems.at[sem_at],
            recv_sem=sems.at[sem_at + 1],
            device_id=peer,
            device_id_type=pl.DeviceIdType.MESH,
        ).start()

    def across(g, c):
        fetch(g).wait()
        rows = pl.ds(pl.multiple_of(g * 16, 16), 16)
        place = pl.multiple_of(lax.rem(g, 6) * 16, 16)
        total = jnp.zeros((256, 256), jnp.float32)
        lane = lax.broadcasted_iota(jnp.int32, (16, 128), 1)
        for t in range(6):
            lo, hi = t * 1664, (t + 1) * 1664
            real = data[0, rows, lo:hi].astype(jnp.float32)
            other = data[1, rows, lo:hi].astype(jnp.float32)
            parts = []
            for h in range(2):
                both = jnp.concatenate(
                    [real[h * 8 : h * 8 + 8], other[h * 8 : h * 8 + 8]], axis=0
                ).astype(jnp.bfloat16)
                pieces = []
                for a in range(16):
                    tile, off = divmod(a * 104, 128)
                    piece = both[:, tile * 128 : tile * 128 + 128]
                    if off > 24:
                        piece = jnp.where(lane >= off, piece, both[:, tile * 128 + 128 : tile * 128 + 256])
                    if off:
                        piece = pltpu.roll(piece, 128 - off, axis=1)
                    pieces.append(piece)
                parts.append(jnp.concatenate(pieces, axis=0))
            total = total + jnp.dot(
                across_tab[:, t * 256 : (t + 1) * 256],
                jnp.concatenate(parts, axis=1),
                preferred_element_type=jnp.float32,
            )
        image = total[:128] + total[128:]
        for j in range(XW):
            real = jnp.concatenate([image[j * 16 : j * 16 + 8, h * 128 : h * 128 + 128] for h in range(2)], axis=0)
            other = jnp.concatenate([image[j * 16 + 8 : j * 16 + 16, h * 128 : h * 128 + 128] for h in range(2)], axis=0)
            for part, pair in ((0, (real, -other)), (1, (other, real))):
                value = jnp.concatenate(pair, axis=1)
                high = value.astype(jnp.bfloat16)
                low = (value - high.astype(jnp.float32)).astype(jnp.bfloat16)
                at = pl.ds(place + ((j % 2) * 192 + part * 96), 16)
                spec_hi[j // 2, at, :] = high
                spec_lo[j // 2, at, :] = low
        return c

    def down(f):
        for jp in range(4):
            dims = (((1,), (1,)), ((), ()))
            first = lax.dot_general(down_tab[...], spec_hi[jp], dims, preferred_element_type=jnp.float32)
            second = lax.dot_general(down_tab[:128, :], spec_lo[jp], dims, preferred_element_type=jnp.float32)
            planes = (first[:128] + first[128:] + second).astype(jnp.bfloat16)
            for s in range(4):
                sent[f, s, jp * 32 : jp * 32 + 32, :] = planes[s * 32 : s * 32 + 32]

    across_copy.wait()
    for f in range(2):
        lax.fori_loop(6 * f, 6 * f + 6, across, 0)
        if f == 0:
            down_copy.wait()
        down(f)
        if f == 0:
            pl.semaphore_wait(barrier, 38)
        for s in range(4):
            send(sent.at[f, s], got.at[f, slab], 2 * f, (mirror, s))
    depth_copy.wait()
    sens_copy.wait()
    mine = pl.multiple_of(me * 16, 16)
    for f in range(2):
        wait_bytes(got.at[f], sems.at[2 * f + 1])
        for j2 in range(2):
            total = None
            for q in range(4):
                window = got[f, q, :, j2 * 128 : j2 * 128 + 256]
                for h in range(2):
                    term = jnp.dot(
                        window,
                        depth[h, q, 64 - 64 * j2 : 320 - 64 * j2, :],
                        preferred_element_type=jnp.float32,
                    )
                    total = term if total is None else total + term
            acc[...] = total
            for jp in range(4):
                j = jp * 2 + j2
                real = other = None
                for coil in range(4):
                    wave_real = acc[jp * 32 : jp * 32 + 26, coil * 256 : coil * 256 + 96]
                    wave_other = acc[jp * 32 : jp * 32 + 26, coil * 256 + 128 : coil * 256 + 224]
                    sens_real = sens[0, coil, pl.ds(j, 26, stride=8), :]
                    sens_other = sens[1, coil, pl.ds(j, 26, stride=8), :]
                    term_real = sens_real * wave_real + sens_other * wave_other
                    term_other = sens_real * wave_other - sens_other * wave_real
                    real = term_real if real is None else real + term_real
                    other = term_other if other is None else other + term_other
                pad = ((0, 0), (0, 32))
                frames[f, pl.ds(j, 26, stride=16), :] = jnp.pad(real, pad)
                frames[f, pl.ds(j + 8, 26, stride=16), :] = jnp.pad(other, pad)

        def scatter(k, c, f=f):
            peer = tm_peer(k)

            @pl.when(peer[0] < ROWS)
            def _():
                first = pl.multiple_of(peer[0] * 16, 16)
                send(frames.at[f, pl.ds(first, 16), :], recv.at[2 * mirror + f], 4, peer)

            return c

        lax.fori_loop(1, 32, scatter, 0)

    for f in range(2):
        wait_bytes(sent.at[f], sems.at[2 * f])

    @pl.when(me < ROWS)
    def _():
        for f in range(2):
            recv[2 * mirror + f] = frames[f, pl.ds(mine, 16), :]
        wait_bytes(frames.at[:, pl.ds(0, (ROWS - 1) * 16), :], sems.at[4])
        wait_bytes(recv.at[pl.ds(0, 62)], sems.at[5])
        flat = recv.reshape(FRAMES * 16, 128)
        for i in range(16):
            whole[:, i * 128 : (i + 1) * 128] = flat[pl.ds(i, FRAMES, stride=16), :]

    @pl.when(me >= ROWS)
    def _():
        wait_bytes(frames.at[:, pl.ds(0, ROWS * 16), :], sems.at[4])
        whole[...] = jnp.zeros_like(whole)

    gram = dot_t(whole[...], whole[...])
    packed = jnp.concatenate([gram[:32], gram[32:]], axis=1)

    def all_sum(value, buf, pos, count, peer_of, sem_at):
        buf[pl.ds(pos, 1)] = value[None]

        def tell(k, c):
            send(buf.at[pl.ds(pos, 1)], buf.at[pl.ds(pos, 1)], sem_at, peer_of(k))
            return c

        lax.fori_loop(1, count, tell, 0)
        wait_bytes(buf.at[pl.ds(0, count - 1)], sems.at[sem_at])
        wait_bytes(buf.at[pl.ds(0, count - 1)], sems.at[sem_at + 1])
        total = buf[0]
        for k in range(1, count):
            total = total + buf[k]
        return total

    packed = all_sum(packed, gyz, yz_pos, 16, yz_peer, 6)
    packed = all_sum(packed, gx, x_pos, 8, x_peer, 8)
    gram = jnp.concatenate([packed[:, :64], packed[:, 64:]], axis=0)
    image, coeff = root_coefficients(gram)
    mixing = lax.dot_general(
        image,
        coeff,
        (((0,), (0,)), ((), ())),
        precision=lax.Precision.HIGHEST,
        preferred_element_type=jnp.float32,
    )

    @pl.when(me < ROWS)
    def _():
        for i in range(16):
            outf[pl.ds(i, FRAMES, stride=16), :] = matmul(mixing, whole[:, i * 128 : (i + 1) * 128])
        outb[...] = outf[...].reshape(FRAMES, 16, 128).astype(jnp.bfloat16)

        def give(k, c):
            peer = tm_peer(k)
            send(outb.at[pl.ds(2 * peer[0], 2)], out_ref.at[:, pl.ds(mine, 16), :], 10, peer)
            return c

        lax.fori_loop(1, 32, give, 0)
        out_ref[:, pl.ds(mine, 16), :] = outb[pl.ds(2 * me, 2)]
        wait_bytes(outb.at[pl.ds(0, 62)], sems.at[10])
        wait_bytes(out_ref.at[:, pl.ds(0, (ROWS - 1) * 16), :], sems.at[11])

    @pl.when(me >= ROWS)
    def _():
        wait_bytes(out_ref, sems.at[11])


def local(kspace, sens):
    hbm = pl.BlockSpec(memory_space=pltpu.HBM)
    projected = pl.pallas_call(
        kernel,
        out_shape=jax.ShapeDtypeStruct((2, ROWS * 16, 128), jnp.bfloat16),
        in_specs=[hbm] * 5,
        out_specs=pl.BlockSpec(memory_space=pltpu.VMEM),
        scratch_shapes=[
            pltpu.VMEM((2, 192, 9984), jnp.bfloat16),
            pltpu.VMEM((4, 384, 256), jnp.bfloat16),
            pltpu.VMEM((4, 384, 256), jnp.bfloat16),
            pltpu.VMEM((2, 4, 128, 384), jnp.bfloat16),
            pltpu.VMEM((2, 4, 128, 384), jnp.bfloat16),
            pltpu.VMEM((128, 1024), jnp.float32),
            pltpu.VMEM((2, 4, 208, NZ), jnp.float32),
            pltpu.VMEM((256, 1536), jnp.bfloat16),
            pltpu.VMEM((256, 256), jnp.bfloat16),
            pltpu.VMEM((2, 4, 320, 1024), jnp.bfloat16),
            pltpu.VMEM((2, 512, 128), jnp.float32),
            pltpu.VMEM((FRAMES, 16, 128), jnp.float32),
            pltpu.VMEM((FRAMES, 2048), jnp.float32),
            pltpu.VMEM((FRAMES * 16, 128), jnp.float32),
            pltpu.VMEM((FRAMES, 16, 128), jnp.bfloat16),
            pltpu.VMEM((16, 32, 128), jnp.float32),
            pltpu.VMEM((8, 32, 128), jnp.float32),
            pltpu.SemaphoreType.DMA((12,)),
            pltpu.SemaphoreType.DMA((4,)),
            pltpu.SemaphoreType.DMA((12,)),
        ],
        compiler_params=pltpu.CompilerParams(
            collective_id=0, has_side_effects=True, vmem_limit_bytes=56 * 1024 * 1024
        ),
        name="frames_to_projection",
    )(
        kspace.reshape(2, 192, NX * NY),
        sens.transpose(0, 1, 3, 2, 4).reshape(2, 4, 208, NZ),
        across_table(),
        down_table(),
        depth_table(),
    )
    projected = projected.reshape(2, ROWS, 2, XW, 128)[..., :NZ].astype(jnp.float32)
    return projected.transpose(0, 2, 3, 1, 4)


def solution(mesh):
    in_specs = (P(None, "tm", None, "slab", None), P(None, None, None, "slab", None))
    out_specs = P("tm", None, None, "slab", None)
    return jax.shard_map(local, mesh=mesh, in_specs=in_specs, out_specs=out_specs, check_vma=False)
```

```python
import jax
import jax.numpy as jnp
import ml_dtypes
import numpy as np
from jax import lax
from jax.experimental import pallas as pl
from jax.experimental.pallas import tpu as pltpu
from jax.sharding import PartitionSpec as P

NX = 96
NY = 104
NZ = 96
RANK = 32
ITERS = 4
XW = 8
FRAMES = 64
ROWS = NY // 4
PANEL = 16


def matmul(left, right):
    return jnp.dot(
        left, right, precision=lax.Precision.HIGHEST, preferred_element_type=jnp.float32
    )


def dot_t(left, right):
    return lax.dot_general(
        left,
        right,
        (((1,), (1,)), ((), ())),
        precision=lax.Precision.HIGHEST,
        preferred_element_type=jnp.float32,
    )


def wait_bytes(ref, sem):
    pltpu.make_async_copy(ref, ref, sem).wait()


def eliminate(tables):
    tables = list(tables)
    row = lax.broadcasted_iota(jnp.int32, (RANK, 128), 0)
    lane = lax.broadcasted_iota(jnp.int32, (RANK, 128), 1)
    for k in range(0, RANK, PANEL):
        columns = [
            jnp.broadcast_to(tables[0][:, k + m : k + m + 1], (RANK, 128)) for m in range(PANEL)
        ]
        rows = [[table[k + m : k + m + 1, :] for m in range(PANEL)] for table in tables]
        for m in range(PANEL):
            inverse = 1.0 / columns[m][k + m : k + m + 1, :]
            factor = jnp.where(row > k + m, columns[m] * inverse, 0.0)
            for n in range(m + 1, PANEL):
                columns[n] = columns[n] - factor * columns[n][k + m : k + m + 1, :]
                for held in rows:
                    held[n] = held[n] - factor[k + n : k + n + 1, :] * held[m]
            for i, held in enumerate(rows):
                tables[i] = tables[i] - factor * held[m]
    diagonal = jnp.sum(jnp.where(lane == row, tables[0], 0.0), axis=1, keepdims=True)
    scale = lax.rsqrt(diagonal)
    return [table * scale for table in tables]


def root_coefficients(gram):
    pad = jnp.zeros((RANK, 32), jnp.float32)
    image = gram[:RANK] + gram[RANK:]
    inner = image[:, :RANK] + image[:, RANK:]
    for sweep in range(ITERS):
        (table,) = eliminate([jnp.concatenate([inner, image, pad], axis=1)])
        weights = table[:, RANK : RANK + FRAMES]
        image = matmul(weights, gram)
        inner = dot_t(image, weights)
    table, extra = eliminate(
        [
            jnp.concatenate([inner, image, pad], axis=1),
            jnp.concatenate([weights, pad, pad], axis=1),
        ]
    )
    return table[:, RANK : RANK + FRAMES], extra[:, :FRAMES]


def split_bf16(table):
    high = table.astype(ml_dtypes.bfloat16)
    low = (table - high.astype(np.float64)).astype(ml_dtypes.bfloat16)
    return high, low


def across_table():
    x = np.arange(XW) + (NX - XW) // 2
    angle = 2.0 * np.pi * (x[:, None] * np.arange(NX)[None, :] % NX) / NX
    cos, sin = np.cos(angle) / np.sqrt(NX), np.sin(angle) / np.sqrt(NX)
    table = np.zeros((XW, 2, 8, NX, 2, 8))
    for r in range(8):
        table[:, 0, r, :, 0, r] = cos
        table[:, 0, r, :, 1, r] = -sin
        table[:, 1, r, :, 0, r] = sin
        table[:, 1, r, :, 1, r] = cos
    return np.concatenate(split_bf16(table.reshape(XW * 16, NX * 16)), axis=0)


def down_table():
    angle = 2.0 * np.pi * (np.arange(NY)[:, None] * np.arange(NY)[None, :] % NY) / NY
    table = np.zeros((4, 32, 2, 128))
    table[:, :26, 0, :NY] = np.cos(angle).reshape(4, 26, NY) / np.sqrt(NY)
    table[:, :26, 1, :NY] = np.sin(angle).reshape(4, 26, NY) / np.sqrt(NY)
    return np.concatenate(split_bf16(table.reshape(128, 256)), axis=0)


def depth_table():
    angle = 2.0 * np.pi * (np.arange(NZ)[:, None] * np.arange(NZ)[None, :] % NZ) / NZ
    cos = (np.cos(angle) / np.sqrt(NZ)).reshape(4, 24, NZ)
    sin = (np.sin(angle) / np.sqrt(NZ)).reshape(4, 24, NZ)
    table = np.zeros((4, 2, 2, 24, 2, 2, 128))
    for c in range(2):
        table[:, 0, c, :, c, 0, :NZ] = cos
        table[:, 1, c, :, c, 0, :NZ] = -sin
        table[:, 0, c, :, c, 1, :NZ] = sin
        table[:, 1, c, :, c, 1, :NZ] = cos
    full = np.zeros((4, 128, 512))
    full[:, :96] = table.reshape(4, 96, 512)
    return np.stack(split_bf16(full.reshape(512, 512)))


def kernel(
    k_ref, sens_ref, plane_ref, depth_ref, out_ref,
    data, spec_hi, spec_lo, sent, got, acc, sens, plane_tab, depth,
    frames, recv, whole, outf, outb, g_row, g_plane, data_sems, table_sems, sems,
):
    me = lax.axis_index("tm")
    slab = lax.axis_index("slab")
    x_lo = me % 2
    x_pos = slab * 2 + x_lo
    yz_pos = me // 2
    far = lax.rem(slab + 2, 4)

    def tm_peer(k):
        return (lax.rem(me + k, 32), slab)

    def x_peer(k):
        other = lax.rem(x_pos + k, 8)
        return (me - x_lo + other % 2, other // 2)

    def yz_peer(k):
        return (lax.rem(yz_pos + k, 16) * 2 + x_lo, slab)

    def fetch(g):
        rows = pl.ds(pl.multiple_of(g * 16, 16), 16)
        return pltpu.make_async_copy(k_ref.at[:, rows, :], data.at[:, rows, :], data_sems.at[g])

    def begin(g, c):
        fetch(g).start()
        return c

    plane_copy = pltpu.make_async_copy(plane_ref, plane_tab, table_sems.at[0])
    depth_copy = pltpu.make_async_copy(depth_ref, depth, table_sems.at[1])
    sens_copy = pltpu.make_async_copy(sens_ref, sens, table_sems.at[2])
    fetch(0).start()
    plane_copy.start()
    lax.fori_loop(1, 12, begin, 0)
    depth_copy.start()
    sens_copy.start()

    barrier = pltpu.get_barrier_semaphore()

    def greet(peer):
        pl.semaphore_signal(barrier, inc=1, device_id=peer, device_id_type=pl.DeviceIdType.MESH)

    lax.fori_loop(1, 32, lambda k, c: (greet(tm_peer(k)), c)[1], 0)
    lax.fori_loop(1, 8, lambda k, c: (greet(x_peer(k)), c)[1], 0)
    frames[...] = jnp.zeros_like(frames)

    def send(src, dst, sem_at, peer):
        pltpu.make_async_remote_copy(
            src_ref=src,
            dst_ref=dst,
            send_sem=sems.at[sem_at],
            recv_sem=sems.at[sem_at + 1],
            device_id=peer,
            device_id_type=pl.DeviceIdType.MESH,
        ).start()

    def across(g, c):
        fetch(g).wait()
        rows = pl.ds(pl.multiple_of(g * 16, 16), 16)
        place = pl.multiple_of(lax.rem(g, 3) * 16, 16)
        total = jnp.zeros((256, 256), jnp.float32)
        lane = lax.broadcasted_iota(jnp.int32, (16, 128), 1)
        for t in range(6):
            lo, hi = t * 1664, (t + 1) * 1664
            real = data[0, rows, lo:hi].astype(jnp.float32)
            other = data[1, rows, lo:hi].astype(jnp.float32)
            parts = []
            for h in range(2):
                both = jnp.concatenate(
                    [real[h * 8 : h * 8 + 8], other[h * 8 : h * 8 + 8]], axis=0
                ).astype(jnp.bfloat16)
                pieces = []
                for a in range(16):
                    tile, off = divmod(a * 104, 128)
                    piece = both[:, tile * 128 : tile * 128 + 128]
                    if off > 24:
                        piece = jnp.where(lane >= off, piece, both[:, tile * 128 + 128 : tile * 128 + 256])
                    if off:
                        piece = pltpu.roll(piece, 128 - off, axis=1)
                    pieces.append(piece)
                parts.append(jnp.concatenate(pieces, axis=0))
            total = total + jnp.dot(
                plane_tab[:, t * 256 : (t + 1) * 256],
                jnp.concatenate(parts, axis=1),
                preferred_element_type=jnp.float32,
            )
        image = total[:128] + total[128:]
        for j in range(XW):
            real = jnp.concatenate([image[j * 16 : j * 16 + 8, h * 128 : h * 128 + 128] for h in range(2)], axis=0)
            other = jnp.concatenate([image[j * 16 + 8 : j * 16 + 16, h * 128 : h * 128 + 128] for h in range(2)], axis=0)
            for part, pair in ((0, (real, -other)), (1, (other, real))):
                value = jnp.concatenate(pair, axis=1)
                high = value.astype(jnp.bfloat16)
                low = (value - high.astype(jnp.float32)).astype(jnp.bfloat16)
                at = pl.ds(place + ((j % 4) * 96 + part * 48), 16)
                spec_hi[j // 4, at, :] = high
                spec_lo[j // 4, at, :] = low
        return c

    def down(chunk):
        for jq in range(2):
            dims = (((1,), (1,)), ((), ()))
            first = lax.dot_general(plane_tab[:, 1536:], spec_hi[jq], dims, preferred_element_type=jnp.float32)
            second = lax.dot_general(plane_tab[:128, 1536:], spec_lo[jq], dims, preferred_element_type=jnp.float32)
            planes = (first[:128] + first[128:] + second).astype(jnp.bfloat16)
            for s in range(4):
                sent[chunk, s, jq * 32 : jq * 32 + 32, :] = planes[s * 32 : s * 32 + 32]

    plane_copy.wait()
    for chunk in range(4):
        lax.fori_loop(3 * chunk, 3 * chunk + 3, across, 0)
        down(chunk)
        if chunk == 0:
            pl.semaphore_wait(barrier, 38)
        for other in (far, far + 1 - 2 * (slab % 2), slab + 1 - 2 * (slab % 2)):
            send(sent.at[chunk, other], got.at[chunk, slab], 2 * chunk, (me, other))
        got[chunk, pl.ds(slab, 1)] = sent[chunk, pl.ds(slab, 1)]
    depth_copy.wait()
    sens_copy.wait()
    mine = pl.multiple_of(me * 16, 16)
    for chunk in range(4):
        f, pair = divmod(chunk, 2)
        wait_bytes(got.at[chunk, pl.ds(0, 3)], sems.at[2 * chunk + 1])
        lane = lax.broadcasted_iota(jnp.int32, (64, 128), 1)
        blocks = []
        for q in range(4):
            third = [got[chunk, q, :, t * 128 : t * 128 + 128] for t in range(3)]
            pieces = (
                third[0],
                pltpu.roll(jnp.where(lane >= 96, third[0], third[1]), 32, axis=1),
                pltpu.roll(jnp.where(lane >= 64, third[1], third[2]), 64, axis=1),
                pltpu.roll(third[2], 96, axis=1),
            )
            blocks.append(jnp.concatenate(pieces, axis=0))
        gathered = jnp.concatenate(blocks, axis=1)
        acc[...] = jnp.dot(gathered, depth[0], preferred_element_type=jnp.float32) + jnp.dot(
            gathered, depth[1], preferred_element_type=jnp.float32
        )
        for jq in range(2):
            for j4 in range(4):
                j = jq * 4 + j4
                real = other = None
                for c in range(2):
                    rows = slice(j4 * 64 + jq * 32, j4 * 64 + jq * 32 + 26)
                    wave_real = acc[rows, c * 256 : c * 256 + 96]
                    wave_other = acc[rows, c * 256 + 128 : c * 256 + 224]
                    sens_real = sens[0, pair * 2 + c, pl.ds(j, 26, stride=8), :]
                    sens_other = sens[1, pair * 2 + c, pl.ds(j, 26, stride=8), :]
                    term_real = sens_real * wave_real + sens_other * wave_other
                    term_other = sens_real * wave_other - sens_other * wave_real
                    real = term_real if real is None else real + term_real
                    other = term_other if other is None else other + term_other
                pad = ((0, 0), (0, 32))
                real, other = jnp.pad(real, pad), jnp.pad(other, pad)
                at_real, at_other = pl.ds(j, 26, stride=16), pl.ds(j + 8, 26, stride=16)
                if pair:
                    real = real + frames[f, at_real, :]
                    other = other + frames[f, at_other, :]
                frames[f, at_real, :] = real
                frames[f, at_other, :] = other

        def scatter(k, c, f=f):
            peer = tm_peer(k)

            @pl.when(peer[0] < ROWS)
            def _():
                first = pl.multiple_of(peer[0] * 16, 16)
                send(frames.at[f, pl.ds(first, 16), :], recv.at[2 * me + f], 8, peer)

            return c

        if pair:
            lax.fori_loop(1, 32, scatter, 0)

    @pl.when(me < ROWS)
    def _():
        for f in range(2):
            recv[2 * me + f] = frames[f, pl.ds(mine, 16), :]
        wait_bytes(recv.at[pl.ds(0, 62)], sems.at[9])
        flat = recv.reshape(FRAMES * 16, 128)
        for i in range(16):
            value = flat[pl.ds(i, FRAMES, stride=16), :]
            high = value.astype(jnp.bfloat16)
            whole[:FRAMES, i * 128 : (i + 1) * 128] = high
            whole[FRAMES:, i * 128 : (i + 1) * 128] = (value - high.astype(jnp.float32)).astype(jnp.bfloat16)

    @pl.when(me >= ROWS)
    def _():
        whole[...] = jnp.zeros_like(whole)

    quarters = lax.dot_general(
        whole[...], whole[...], (((1,), (1,)), ((), ())), preferred_element_type=jnp.float32
    )
    halves = quarters[:FRAMES] + quarters[FRAMES:]
    gram = halves[:, :FRAMES] + halves[:, FRAMES:]
    packed = jnp.concatenate([gram[:32], gram[32:]], axis=1)

    def tell(slot, sem_at, count, peer_of):
        def one(k, c):
            send(slot, slot, sem_at, peer_of(k))
            return c

        lax.fori_loop(1, count, one, 0)

    def heard(buf, count, sem_at):
        wait_bytes(buf.at[pl.ds(0, count - 1)], sems.at[sem_at])
        wait_bytes(buf.at[pl.ds(0, count - 1)], sems.at[sem_at + 1])

    def summed(buf, count):
        total = buf[0]
        for k in range(1, count):
            total = total + buf[k]
        return total

    g_plane[pl.ds(yz_pos, 1)] = packed[None]
    tell(g_plane.at[pl.ds(yz_pos, 1)], 10, 16, yz_peer)
    for chunk in range(4):
        wait_bytes(sent.at[chunk, pl.ds(0, 3)], sems.at[2 * chunk])

    @pl.when(me < ROWS)
    def _():
        wait_bytes(frames.at[:, pl.ds(0, (ROWS - 1) * 16), :], sems.at[8])

    @pl.when(me >= ROWS)
    def _():
        wait_bytes(frames.at[:, pl.ds(0, ROWS * 16), :], sems.at[8])

    heard(g_plane, 16, 10)
    g_row[pl.ds(x_pos, 1)] = summed(g_plane, 16)[None]
    tell(g_row.at[pl.ds(x_pos, 1)], 12, 8, x_peer)
    heard(g_row, 8, 12)
    packed = summed(g_row, 8)
    gram = jnp.concatenate([packed[:, :64], packed[:, 64:]], axis=0)
    image, coeff = root_coefficients(gram)
    mixing = lax.dot_general(
        image,
        coeff,
        (((0,), (0,)), ((), ())),
        precision=lax.Precision.HIGHEST,
        preferred_element_type=jnp.float32,
    )

    @pl.when(me < ROWS)
    def _():
        high = mixing.astype(jnp.bfloat16)
        low = (mixing - high.astype(jnp.float32)).astype(jnp.bfloat16)
        left = jnp.concatenate(
            [jnp.concatenate([high, high], axis=1), jnp.concatenate([low, low], axis=1)], axis=0
        )
        for i in range(16):
            both = jnp.dot(
                left, whole[:, i * 128 : (i + 1) * 128], preferred_element_type=jnp.float32
            )
            outf[pl.ds(i, FRAMES, stride=16), :] = both[:FRAMES] + both[FRAMES:]
        outb[...] = outf[...].reshape(FRAMES, 16, 128).astype(jnp.bfloat16)

        def give(k, c):
            peer = tm_peer(k)
            send(outb.at[pl.ds(2 * peer[0], 2)], out_ref.at[:, pl.ds(mine, 16), :], 16, peer)
            return c

        lax.fori_loop(1, 32, give, 0)
        out_ref[:, pl.ds(mine, 16), :] = outb[pl.ds(2 * me, 2)]
        wait_bytes(outb.at[pl.ds(0, 62)], sems.at[16])
        wait_bytes(out_ref.at[:, pl.ds(0, (ROWS - 1) * 16), :], sems.at[17])

    @pl.when(me >= ROWS)
    def _():
        wait_bytes(out_ref, sems.at[17])


def local(kspace, sens):
    hbm = pl.BlockSpec(memory_space=pltpu.HBM)
    projected = pl.pallas_call(
        kernel,
        out_shape=jax.ShapeDtypeStruct((2, ROWS * 16, 128), jnp.bfloat16),
        in_specs=[hbm] * 4,
        out_specs=pl.BlockSpec(memory_space=pltpu.VMEM),
        scratch_shapes=[
            pltpu.VMEM((2, 192, 9984), jnp.bfloat16),
            pltpu.VMEM((2, 384, 256), jnp.bfloat16),
            pltpu.VMEM((2, 384, 256), jnp.bfloat16),
            pltpu.VMEM((4, 4, 64, 384), jnp.bfloat16),
            pltpu.VMEM((4, 4, 64, 384), jnp.bfloat16),
            pltpu.VMEM((256, 512), jnp.float32),
            pltpu.VMEM((2, 4, 208, NZ), jnp.float32),
            pltpu.VMEM((256, 1792), jnp.bfloat16),
            pltpu.VMEM((2, 512, 512), jnp.bfloat16),
            pltpu.VMEM((2, 512, 128), jnp.float32),
            pltpu.VMEM((FRAMES, 16, 128), jnp.float32),
            pltpu.VMEM((2 * FRAMES, 2048), jnp.bfloat16),
            pltpu.VMEM((FRAMES * 16, 128), jnp.float32),
            pltpu.VMEM((FRAMES, 16, 128), jnp.bfloat16),
            pltpu.VMEM((8, 32, 128), jnp.float32),
            pltpu.VMEM((16, 32, 128), jnp.float32),
            pltpu.SemaphoreType.DMA((12,)),
            pltpu.SemaphoreType.DMA((3,)),
            pltpu.SemaphoreType.DMA((18,)),
        ],
        compiler_params=pltpu.CompilerParams(
            collective_id=0, has_side_effects=True, vmem_limit_bytes=54784 * 1024
        ),
        name="frames_to_projection",
    )(
        kspace.reshape(2, 192, NX * NY),
        sens.transpose(0, 1, 3, 2, 4).reshape(2, 4, 208, NZ),
        np.concatenate([across_table(), down_table()], axis=1),
        depth_table(),
    )
    projected = projected.reshape(2, ROWS, 2, XW, 128)[..., :NZ].astype(jnp.float32)
    return projected.transpose(0, 2, 3, 1, 4)


def solution(mesh):
    in_specs = (P(None, "tm", None, "slab", None), P(None, None, None, "slab", None))
    out_specs = P("tm", None, None, "slab", None)
    return jax.shard_map(local, mesh=mesh, in_specs=in_specs, out_specs=out_specs, check_vma=False)
```

```python
import jax
import jax.numpy as jnp
import ml_dtypes
import numpy as np
from jax import lax
from jax.experimental import pallas as pl
from jax.experimental.pallas import tpu as pltpu
from jax.sharding import PartitionSpec as P

NX = 96
NY = 104
NZ = 96
RANK = 32
ITERS = 4
XW = 8
FRAMES = 64
ROWS = NY // 4
PANEL = 16


def matmul(left, right):
    return jnp.dot(
        left, right, precision=lax.Precision.HIGHEST, preferred_element_type=jnp.float32
    )


def dot_t(left, right):
    return lax.dot_general(
        left,
        right,
        (((1,), (1,)), ((), ())),
        precision=lax.Precision.HIGHEST,
        preferred_element_type=jnp.float32,
    )


def wait_bytes(ref, sem):
    pltpu.make_async_copy(ref, ref, sem).wait()


def eliminate(tables):
    tables = list(tables)
    row = lax.broadcasted_iota(jnp.int32, (RANK, 128), 0)
    lane = lax.broadcasted_iota(jnp.int32, (RANK, 128), 1)
    for k in range(0, RANK, PANEL):
        columns = [
            jnp.broadcast_to(tables[0][:, k + m : k + m + 1], (RANK, 128)) for m in range(PANEL)
        ]
        rows = [[table[k + m : k + m + 1, :] for m in range(PANEL)] for table in tables]
        for m in range(PANEL):
            inverse = 1.0 / columns[m][k + m : k + m + 1, :]
            factor = jnp.where(row > k + m, columns[m] * inverse, 0.0)
            for n in range(m + 1, PANEL):
                columns[n] = columns[n] - factor * columns[n][k + m : k + m + 1, :]
                for held in rows:
                    held[n] = held[n] - factor[k + n : k + n + 1, :] * held[m]
            for i, held in enumerate(rows):
                tables[i] = tables[i] - factor * held[m]
    diagonal = jnp.sum(jnp.where(lane == row, tables[0], 0.0), axis=1, keepdims=True)
    scale = lax.rsqrt(diagonal)
    return [table * scale for table in tables]


def root_coefficients(gram):
    pad = jnp.zeros((RANK, 32), jnp.float32)
    image = gram[:RANK] + gram[RANK:]
    inner = image[:, :RANK] + image[:, RANK:]
    for sweep in range(ITERS):
        (table,) = eliminate([jnp.concatenate([inner, image, pad], axis=1)])
        weights = table[:, RANK : RANK + FRAMES]
        image = matmul(weights, gram)
        inner = dot_t(image, weights)
    table, extra = eliminate(
        [
            jnp.concatenate([inner, image, pad], axis=1),
            jnp.concatenate([weights, pad, pad], axis=1),
        ]
    )
    return table[:, RANK : RANK + FRAMES], extra[:, :FRAMES]


def split_bf16(table):
    high = table.astype(ml_dtypes.bfloat16)
    low = (table - high.astype(np.float64)).astype(ml_dtypes.bfloat16)
    return high, low


def across_table():
    x = np.arange(XW) + (NX - XW) // 2
    angle = 2.0 * np.pi * (x[:, None] * np.arange(NX)[None, :] % NX) / NX
    cos, sin = np.cos(angle) / np.sqrt(NX), np.sin(angle) / np.sqrt(NX)
    table = np.zeros((XW, 2, 8, NX, 2, 8))
    for r in range(8):
        table[:, 0, r, :, 0, r] = cos
        table[:, 0, r, :, 1, r] = -sin
        table[:, 1, r, :, 0, r] = sin
        table[:, 1, r, :, 1, r] = cos
    return np.concatenate(split_bf16(table.reshape(XW * 16, NX * 16)), axis=0)


def down_table():
    angle = 2.0 * np.pi * (np.arange(NY)[:, None] * np.arange(NY)[None, :] % NY) / NY
    table = np.zeros((4, 32, 2, 128))
    table[:, :26, 0, :NY] = np.cos(angle).reshape(4, 26, NY) / np.sqrt(NY)
    table[:, :26, 1, :NY] = np.sin(angle).reshape(4, 26, NY) / np.sqrt(NY)
    return np.concatenate(split_bf16(table.reshape(128, 256)), axis=0)


def depth_table():
    angle = 2.0 * np.pi * (np.arange(NZ)[:, None] * np.arange(NZ)[None, :] % NZ) / NZ
    cos = (np.cos(angle) / np.sqrt(NZ)).reshape(4, 24, NZ)
    sin = (np.sin(angle) / np.sqrt(NZ)).reshape(4, 24, NZ)
    table = np.zeros((4, 2, 2, 24, 2, 2, 128))
    for c in range(2):
        table[:, 0, c, :, c, 0, :NZ] = cos
        table[:, 1, c, :, c, 0, :NZ] = -sin
        table[:, 0, c, :, c, 1, :NZ] = sin
        table[:, 1, c, :, c, 1, :NZ] = cos
    full = np.zeros((4, 128, 512))
    full[:, :96] = table.reshape(4, 96, 512)
    return np.stack(split_bf16(full.reshape(512, 512)))


def kernel(
    k_ref, sens_ref, plane_ref, depth_ref, out_ref,
    data, spec_hi, spec_lo, sent, got, acc, sens, plane_tab, depth,
    frames, recv, whole, outf, outb, g_row, g_plane, data_sems, table_sems, sems,
):
    me = lax.axis_index("tm")
    slab = lax.axis_index("slab")
    x_lo = me % 2
    x_pos = slab * 2 + x_lo
    yz_pos = me // 2
    far = lax.rem(slab + 2, 4)

    def tm_peer(k):
        return (lax.rem(me + k, 32), slab)

    def x_peer(k):
        other = lax.rem(x_pos + k, 8)
        return (me - x_lo + other % 2, other // 2)

    def yz_peer(k):
        return (lax.rem(yz_pos + k, 16) * 2 + x_lo, slab)

    def fetch(g):
        rows = pl.ds(pl.multiple_of(g * 16, 16), 16)
        return pltpu.make_async_copy(k_ref.at[:, rows, :], data.at[:, rows, :], data_sems.at[g])

    def begin(g, c):
        fetch(g).start()
        return c

    plane_copy = pltpu.make_async_copy(plane_ref, plane_tab, table_sems.at[0])
    depth_copy = pltpu.make_async_copy(depth_ref, depth, table_sems.at[1])
    sens_copy = pltpu.make_async_copy(sens_ref, sens, table_sems.at[2])
    fetch(0).start()
    plane_copy.start()
    lax.fori_loop(1, 3, begin, 0)
    barrier = pltpu.get_barrier_semaphore()

    def greet(peer):
        pl.semaphore_signal(barrier, inc=1, device_id=peer, device_id_type=pl.DeviceIdType.MESH)

    lax.fori_loop(1, 32, lambda k, c: (greet(tm_peer(k)), c)[1], 0)
    lax.fori_loop(1, 8, lambda k, c: (greet(x_peer(k)), c)[1], 0)
    lax.fori_loop(3, 12, begin, 0)
    depth_copy.start()
    sens_copy.start()

    frames[...] = jnp.zeros_like(frames)

    def send(src, dst, sem_at, peer):
        pltpu.make_async_remote_copy(
            src_ref=src,
            dst_ref=dst,
            send_sem=sems.at[sem_at],
            recv_sem=sems.at[sem_at + 1],
            device_id=peer,
            device_id_type=pl.DeviceIdType.MESH,
        ).start()

    def across(g, c):
        fetch(g).wait()
        rows = pl.ds(pl.multiple_of(g * 16, 16), 16)
        place = pl.multiple_of(lax.rem(g, 3) * 16, 16)
        total = jnp.zeros((256, 256), jnp.float32)
        lane = lax.broadcasted_iota(jnp.int32, (16, 128), 1)
        for t in range(6):
            lo, hi = t * 1664, (t + 1) * 1664
            real = data[0, rows, lo:hi].astype(jnp.float32)
            other = data[1, rows, lo:hi].astype(jnp.float32)
            parts = []
            for h in range(2):
                both = jnp.concatenate(
                    [real[h * 8 : h * 8 + 8], other[h * 8 : h * 8 + 8]], axis=0
                ).astype(jnp.bfloat16)
                pieces = []
                for a in range(16):
                    tile, off = divmod(a * 104, 128)
                    piece = both[:, tile * 128 : tile * 128 + 128]
                    if off > 24:
                        piece = jnp.where(lane >= off, piece, both[:, tile * 128 + 128 : tile * 128 + 256])
                    if off:
                        piece = pltpu.roll(piece, 128 - off, axis=1)
                    pieces.append(piece)
                parts.append(jnp.concatenate(pieces, axis=0))
            total = total + jnp.dot(
                plane_tab[:, t * 256 : (t + 1) * 256],
                jnp.concatenate(parts, axis=1),
                preferred_element_type=jnp.float32,
            )
        image = total[:128] + total[128:]
        for j in range(XW):
            real = jnp.concatenate([image[j * 16 : j * 16 + 8, h * 128 : h * 128 + 128] for h in range(2)], axis=0)
            other = jnp.concatenate([image[j * 16 + 8 : j * 16 + 16, h * 128 : h * 128 + 128] for h in range(2)], axis=0)
            for part, pair in ((0, (real, -other)), (1, (other, real))):
                value = jnp.concatenate(pair, axis=1)
                high = value.astype(jnp.bfloat16)
                low = (value - high.astype(jnp.float32)).astype(jnp.bfloat16)
                at = pl.ds(place + ((j % 4) * 96 + part * 48), 16)
                spec_hi[j // 4, at, :] = high
                spec_lo[j // 4, at, :] = low
        return c

    def down(chunk):
        for jq in range(2):
            dims = (((1,), (1,)), ((), ()))
            first = lax.dot_general(plane_tab[:, 1536:], spec_hi[jq], dims, preferred_element_type=jnp.float32)
            second = lax.dot_general(plane_tab[:128, 1536:], spec_lo[jq], dims, preferred_element_type=jnp.float32)
            planes = (first[:128] + first[128:] + second).astype(jnp.bfloat16)
            for s in range(4):
                sent[chunk, s, jq * 32 : jq * 32 + 32, :] = planes[s * 32 : s * 32 + 32]

    plane_copy.wait()
    for chunk in range(4):
        lax.fori_loop(3 * chunk, 3 * chunk + 3, across, 0)
        down(chunk)
        if chunk == 0:
            pl.semaphore_wait(barrier, 38)
        for other in (far, far + 1 - 2 * (slab % 2), slab + 1 - 2 * (slab % 2)):
            send(sent.at[chunk, other], got.at[chunk, slab], 2 * chunk, (me, other))
        got[chunk, pl.ds(slab, 1)] = sent[chunk, pl.ds(slab, 1)]
    depth_copy.wait()
    sens_copy.wait()
    mine = pl.multiple_of(me * 16, 16)
    for chunk in range(4):
        f, pair = divmod(chunk, 2)
        wait_bytes(got.at[chunk, pl.ds(0, 3)], sems.at[2 * chunk + 1])
        lane = lax.broadcasted_iota(jnp.int32, (64, 128), 1)
        blocks = []
        for q in range(4):
            third = [got[chunk, q, :, t * 128 : t * 128 + 128] for t in range(3)]
            pieces = (
                third[0],
                pltpu.roll(jnp.where(lane >= 96, third[0], third[1]), 32, axis=1),
                pltpu.roll(jnp.where(lane >= 64, third[1], third[2]), 64, axis=1),
                pltpu.roll(third[2], 96, axis=1),
            )
            blocks.append(jnp.concatenate(pieces, axis=0))
        gathered = jnp.concatenate(blocks, axis=1)
        acc[...] = jnp.dot(gathered, depth[0], preferred_element_type=jnp.float32) + jnp.dot(
            gathered, depth[1], preferred_element_type=jnp.float32
        )
        for jq in range(2):
            for j4 in range(4):
                j = jq * 4 + j4
                real = other = None
                for c in range(2):
                    rows = slice(j4 * 64 + jq * 32, j4 * 64 + jq * 32 + 26)
                    wave_real = acc[rows, c * 256 : c * 256 + 96]
                    wave_other = acc[rows, c * 256 + 128 : c * 256 + 224]
                    sens_real = sens[0, pair * 2 + c, pl.ds(j, 26, stride=8), :]
                    sens_other = sens[1, pair * 2 + c, pl.ds(j, 26, stride=8), :]
                    term_real = sens_real * wave_real + sens_other * wave_other
                    term_other = sens_real * wave_other - sens_other * wave_real
                    real = term_real if real is None else real + term_real
                    other = term_other if other is None else other + term_other
                pad = ((0, 0), (0, 32))
                real, other = jnp.pad(real, pad), jnp.pad(other, pad)
                at_real, at_other = pl.ds(j, 26, stride=16), pl.ds(j + 8, 26, stride=16)
                if pair:
                    real = real + frames[f, at_real, :]
                    other = other + frames[f, at_other, :]
                frames[f, at_real, :] = real
                frames[f, at_other, :] = other

        def scatter(k, c, f=f):
            peer = tm_peer(k)

            @pl.when(peer[0] < ROWS)
            def _():
                first = pl.multiple_of(peer[0] * 16, 16)
                send(frames.at[f, pl.ds(first, 16), :], recv.at[2 * me + f], 8, peer)

            return c

        if pair:
            lax.fori_loop(1, 32, scatter, 0)

    @pl.when(me < ROWS)
    def _():
        for f in range(2):
            recv[2 * me + f] = frames[f, pl.ds(mine, 16), :]
        wait_bytes(recv.at[pl.ds(0, 62)], sems.at[9])
        flat = recv.reshape(FRAMES * 16, 128)
        for i in range(16):
            value = flat[pl.ds(i, FRAMES, stride=16), :]
            high = value.astype(jnp.bfloat16)
            whole[:FRAMES, i * 128 : (i + 1) * 128] = high
            whole[FRAMES:, i * 128 : (i + 1) * 128] = (value - high.astype(jnp.float32)).astype(jnp.bfloat16)

    @pl.when(me >= ROWS)
    def _():
        whole[...] = jnp.zeros_like(whole)

    quarters = lax.dot_general(
        whole[...], whole[...], (((1,), (1,)), ((), ())), preferred_element_type=jnp.float32
    )
    halves = quarters[:FRAMES] + quarters[FRAMES:]
    gram = halves[:, :FRAMES] + halves[:, FRAMES:]
    packed = jnp.concatenate([gram[:32], gram[32:]], axis=1)

    def tell(slot, sem_at, count, peer_of):
        def one(k, c):
            send(slot, slot, sem_at, peer_of(k))
            return c

        lax.fori_loop(1, count, one, 0)

    def heard(buf, count, sem_at):
        wait_bytes(buf.at[pl.ds(0, count - 1)], sems.at[sem_at])
        wait_bytes(buf.at[pl.ds(0, count - 1)], sems.at[sem_at + 1])

    def summed(buf, count):
        total = buf[0]
        for k in range(1, count):
            total = total + buf[k]
        return total

    g_row[pl.ds(x_pos, 1)] = packed[None]
    tell(g_row.at[pl.ds(x_pos, 1)], 12, 8, x_peer)
    for chunk in range(4):
        wait_bytes(sent.at[chunk, pl.ds(0, 3)], sems.at[2 * chunk])

    @pl.when(me < ROWS)
    def _():
        wait_bytes(frames.at[:, pl.ds(0, (ROWS - 1) * 16), :], sems.at[8])

    @pl.when(me >= ROWS)
    def _():
        wait_bytes(frames.at[:, pl.ds(0, ROWS * 16), :], sems.at[8])

    heard(g_row, 8, 12)
    g_plane[pl.ds(yz_pos, 1)] = summed(g_row, 8)[None]
    tell(g_plane.at[pl.ds(yz_pos, 1)], 10, 16, yz_peer)
    heard(g_plane, 16, 10)
    packed = summed(g_plane, 16)
    gram = jnp.concatenate([packed[:, :64], packed[:, 64:]], axis=0)
    image, coeff = root_coefficients(gram)
    mixing = lax.dot_general(
        image,
        coeff,
        (((0,), (0,)), ((), ())),
        precision=lax.Precision.HIGHEST,
        preferred_element_type=jnp.float32,
    )

    @pl.when(me < ROWS)
    def _():
        high = mixing.astype(jnp.bfloat16)
        low = (mixing - high.astype(jnp.float32)).astype(jnp.bfloat16)
        left = jnp.concatenate(
            [jnp.concatenate([high, high], axis=1), jnp.concatenate([low, low], axis=1)], axis=0
        )
        for i in range(16):
            both = jnp.dot(
                left, whole[:, i * 128 : (i + 1) * 128], preferred_element_type=jnp.float32
            )
            outf[pl.ds(i, FRAMES, stride=16), :] = both[:FRAMES] + both[FRAMES:]
        outb[...] = outf[...].reshape(FRAMES, 16, 128).astype(jnp.bfloat16)

        def give(k, c):
            peer = tm_peer(k)
            send(outb.at[pl.ds(2 * peer[0], 2)], out_ref.at[:, pl.ds(mine, 16), :], 16, peer)
            return c

        lax.fori_loop(1, 32, give, 0)
        out_ref[:, pl.ds(mine, 16), :] = outb[pl.ds(2 * me, 2)]
        wait_bytes(outb.at[pl.ds(0, 62)], sems.at[16])
        wait_bytes(out_ref.at[:, pl.ds(0, (ROWS - 1) * 16), :], sems.at[17])

    @pl.when(me >= ROWS)
    def _():
        wait_bytes(out_ref, sems.at[17])


def local(kspace, sens):
    hbm = pl.BlockSpec(memory_space=pltpu.HBM)
    projected = pl.pallas_call(
        kernel,
        out_shape=jax.ShapeDtypeStruct((2, ROWS * 16, 128), jnp.bfloat16),
        in_specs=[hbm] * 4,
        out_specs=pl.BlockSpec(memory_space=pltpu.VMEM),
        scratch_shapes=[
            pltpu.VMEM((2, 192, 9984), jnp.bfloat16),
            pltpu.VMEM((2, 384, 256), jnp.bfloat16),
            pltpu.VMEM((2, 384, 256), jnp.bfloat16),
            pltpu.VMEM((4, 4, 64, 384), jnp.bfloat16),
            pltpu.VMEM((4, 4, 64, 384), jnp.bfloat16),
            pltpu.VMEM((256, 512), jnp.float32),
            pltpu.VMEM((2, 4, 208, NZ), jnp.float32),
            pltpu.VMEM((256, 1792), jnp.bfloat16),
            pltpu.VMEM((2, 512, 512), jnp.bfloat16),
            pltpu.VMEM((2, 512, 128), jnp.float32),
            pltpu.VMEM((FRAMES, 16, 128), jnp.float32),
            pltpu.VMEM((2 * FRAMES, 2048), jnp.bfloat16),
            pltpu.VMEM((FRAMES * 16, 128), jnp.float32),
            pltpu.VMEM((FRAMES, 16, 128), jnp.bfloat16),
            pltpu.VMEM((8, 32, 128), jnp.float32),
            pltpu.VMEM((16, 32, 128), jnp.float32),
            pltpu.SemaphoreType.DMA((12,)),
            pltpu.SemaphoreType.DMA((3,)),
            pltpu.SemaphoreType.DMA((18,)),
        ],
        compiler_params=pltpu.CompilerParams(
            collective_id=0, has_side_effects=True, vmem_limit_bytes=54784 * 1024
        ),
        name="frames_to_projection",
    )(
        kspace.reshape(2, 192, NX * NY),
        sens.transpose(0, 1, 3, 2, 4).reshape(2, 4, 208, NZ),
        np.concatenate([across_table(), down_table()], axis=1),
        depth_table(),
    )
    projected = projected.reshape(2, ROWS, 2, XW, 128)[..., :NZ].astype(jnp.float32)
    return projected.transpose(0, 2, 3, 1, 4)


def solution(mesh):
    in_specs = (P(None, "tm", None, "slab", None), P(None, None, None, "slab", None))
    out_specs = P("tm", None, None, "slab", None)
    return jax.shard_map(local, mesh=mesh, in_specs=in_specs, out_specs=out_specs, check_vma=False)
```
